32 devices in a mesh: section: 2 (over x), batch: 16 (over z, y, core).
Axes of the slice: x: 2, y: 2, z: 4, core: 2. Of those that a mesh axis runs over, the one named last changes fastest.
Arguments:
- inputs: bfloat16 [32, 512, 192], P('batch'), may hold values from -6 to 6
- segment_ids: int32 [32, 512], P('batch'), may hold values from 0 to 3, never falling along the last dimension, each value on 1 to 256 neighbouring positions
- cotangent: float32 [32, 512, 192], P('batch'), may hold values from -6 to 6
- qkv_master: float32 [2, 110592], P('section', 'batch'), may hold values from -0.4375 to 0.4375
- out_master: float32 [2, 36864], P('section', 'batch'), may hold values from -3.5 to 3.5
- ffn_in_master: float32 [2, 442368], P('section', 'batch'), may hold values from -0.25 to 0.25
- ffn_out_master: float32 [2, 442368], P('section', 'batch'), may hold values from -0.125 to 0.125
- pre_master: float32 [2, 18432], P('section', 'batch'), may hold values from -0.625 to 0.625
- gate_master: float32 [2, 368640], P('section', 'batch'), may hold values from -0.1875 to 0.1875
- skip_master: float32 [2, 36864], P('section', 'batch'), may hold values from -0.4375 to 0.4375
- post_master: float32 [2, 18432], P('section', 'batch'), may hold values from -0.875 to 0.875
- vector_master: float32 [2, 6144], P('section', 'batch'), may hold values from -2 to 2
Outputs:
- layer_outputs: bfloat16 [2, 32, 512, 192], P('section', 'batch')
- input_grads: float32 [2, 32, 512, 192], P('section', 'batch')
- qkv_grad: float32 [2, 110592], P('section', 'batch')
- out_grad: float32 [2, 36864], P('section', 'batch')
- ffn_in_grad: float32 [2, 442368], P('section', 'batch')
- ffn_out_grad: float32 [2, 442368], P('section', 'batch')
- pre_grad: float32 [2, 18432], P('section', 'batch')
- gate_grad: float32 [2, 368640], P('section', 'batch')
- skip_grad: float32 [2, 36864], P('section', 'batch')
- post_grad: float32 [2, 18432], P('section', 'batch')
- vector_grad: float32 [2, 6144], P('section', 'batch')
The draws below stay inside these ranges and needn't reach their ends.
Inputs may be any that keep to these rules, and one draw needn't show every extreme that they name: `segment_ids`: along each row the numbers never fall; all 4 occur, each on 1 to half of 512 frames, one on exactly half.
All inputs are finite; a program needn't handle non-finite values.
Results may differ from the reference program's by a relative error of at most 0.025.
Values may be sent and summed in bfloat16 or wider, within the bound.
No kernel may reach another device: no remote copies, remote signals or barrier semaphores. Data moves between devices by JAX's collectives and lax.ppermute only.
A program may use at most 1.0625 GiB of HBM per device.

```python
import math
import jax
import jax.numpy as jnp
import numpy as np
from jax import lax

H = 192
HEADS = 2
FF = 768
KFF = 3
KWN = 5
WIN = 4
DH = 96
GATES = 384
HALF = 96
ROW = 512
SEGS = 4
ROWS = 32
VCOUNT = 4896
VEC = 6144


def draw_vector_master(key, part):
    key = jax.random.fold_in(key, 7)
    base = jnp.clip(jax.random.normal(key, (2, VEC), jnp.float32), -2.0, 2.0)
    layout = [(H, 0.3, 0.0), (H, 0.3, 0.0), (H, 0.3, 0.0), (H, 0.2, 1.0), (H, 0.3, 0.0), (FF, 0.3, 0.0), (H, 0.3, 0.0), (H, 0.2, 1.0), (H, 0.3, 0.0), (H, 0.3, 0.0), (GATES, 0.3, 0.0), (H, 0.3, 0.0), (HALF, 0.3, 0.0), ((2 * WIN + 1) * DH, 1.0, 0.0), ((2 * WIN + 1) * DH, 1.0, 0.0), (VEC - VCOUNT, 1.0, 0.0)]
    scales = jnp.concatenate([jnp.full((piece[0],), piece[1], jnp.float32) for piece in layout])
    shifts = jnp.concatenate([jnp.full((piece[0],), piece[2], jnp.float32) for piece in layout])
    return base * scales[None, :] + shifts[None, :]


def steps_of(key, shape, split, smallest, high):
    factor_of, own = 1.0, jax.random.fold_in(key, 6)
    for position, parts in split:
        draws = jnp.exp(jax.random.uniform(jax.random.fold_in(own, position), (parts,), jnp.float32, smallest / len(split), high / len(split)))
        factor_of = factor_of * jnp.repeat(draws, shape[position] // parts).reshape([-1 if axis == position else 1 for axis in range(len(shape))])
    return factor_of


def split_up(count, total, reach, slope):
    portions = [(1 << 20) // math.isqrt(standing ** slope) + 1 for standing in range(2, count + 1)]
    spare, given = total - reach - (count - 1), [1] * (count - 1)
    while spare > 0:
        free = [i for i in range(count - 1) if given[i] < reach]
        whole, budget = sum([portions[i] for i in free]), spare
        for i in free:
            addition = min(reach - given[i], max(1, budget * portions[i] // whole), spare)
            given[i] = given[i] + addition
            spare = spare - addition
    return np.array([reach] + given)


def ragged_sizes(stream_key, number_of, total, most, slope):
    if number_of == 2:
        one = jax.random.randint(stream_key, (), max(1, total - most), min(most, total - 1) + 1)
        return jnp.stack([one, total - one])
    sizes = jnp.asarray(split_up(number_of, total, most, slope), jnp.int32)
    couples = (number_of - 1) // 2
    giver, taker = sizes[1:1 + 2 * couples:2], sizes[2:2 + 2 * couples:2]
    slack = jnp.minimum(giver - 1, most - taker)
    moved = jax.random.randint(jax.random.fold_in(stream_key, 1), (couples,), 0, 1 << 20) % (slack + 1)
    sizes = sizes.at[1:1 + 2 * couples:2].set(giver - moved).at[2:2 + 2 * couples:2].set(taker + moved)
    return sizes[jax.random.permutation(jax.random.fold_in(stream_key, 2), number_of)]


def noise(own_key, extent, deviation, reach, split=(), dtype=jnp.bfloat16):
    drawn = jax.random.normal(own_key, extent, jnp.float32) * deviation
    if len(split) > 0:
        drawn = steps_of(own_key, extent, split, -0.22, 0.18) * drawn
    return jnp.clip(drawn, min=-reach, max=reach).astype(dtype)


def setup_inputs(seed: int = 0) -> dict:
    keys = jax.random.split(jax.random.key(seed), 13)
    return {
        "inputs": noise(keys[0], (ROWS, ROW, H), 1.0, 6.0, ((0, 16),)),
        "segment_ids": jax.vmap(lambda own: jnp.searchsorted(jnp.cumsum(ragged_sizes(own, SEGS, ROW, ROW // 2, 1)), jnp.arange(ROW), side="right"))(jax.random.split(keys[1], ROWS)).reshape((ROWS, ROW)).astype(jnp.int32),
        "cotangent": noise(keys[2], (ROWS, ROW, H), 1.0, 6.0, ((0, 16),), jnp.float32),
        "qkv_master": noise(keys[3], (2, 3 * H * H), H ** -0.5, 0.4375, ((0, 2), (1, 16)), jnp.float32),
        "out_master": noise(keys[4], (2, H * H), (max(H // 64, 1)) ** -0.5, 3.5, ((0, 2), (1, 16)), jnp.float32),
        "ffn_in_master": noise(keys[5], (2, KFF * H * FF), (KFF * H) ** -0.5, 0.25, ((0, 2), (1, 16)), jnp.float32),
        "ffn_out_master": noise(keys[6], (2, KFF * FF * H), (KFF * FF) ** -0.5, 0.125, ((0, 2), (1, 16)), jnp.float32),
        "pre_master": noise(keys[7], (2, HALF * H), HALF ** -0.5, 0.625, ((0, 2), (1, 16)), jnp.float32),
        "gate_master": noise(keys[8], (2, KWN * H * GATES), (KWN * H) ** -0.5, 0.1875, ((0, 2), (1, 16)), jnp.float32),
        "skip_master": noise(keys[9], (2, H * H), H ** -0.5, 0.4375, ((0, 2), (1, 16)), jnp.float32),
        "post_master": noise(keys[10], (2, H * HALF), (H // 4) ** -0.5, 0.875, ((0, 2), (1, 16)), jnp.float32),
        "vector_master": draw_vector_master(jax.random.fold_in(keys[12], 71), 0),
    }


highest = lax.Precision.HIGHEST

@jax.custom_vjp
def low(v):
    return lax.optimization_barrier(v.astype(jnp.bfloat16)).astype(jnp.float32)

@jax.custom_vjp
def low_back(v):
    return v

def low_keep(v):
    return (low(v), None)

def low_pass(kept, grad):
    return (grad,)

def back_keep(v):
    return (v, None)

def back_low(kept, grad):
    return (low(grad),)
low.defvjp(low_keep, low_pass)
low_back.defvjp(back_keep, back_low)

def matmul(left_side, right_side):
    return jnp.dot(left_side, right_side, precision=highest)

def vector_parts(vector):
    layout = [('q_bias', H), ('v_bias', H), ('out_bias', H), ('norm1_gain', H), ('norm1_bias', H), ('ffn_bias1', FF), ('ffn_bias2', H), ('norm2_gain', H), ('norm2_bias', H), ('pre_bias', H), ('gate_bias', GATES), ('skip_bias', H), ('post_bias', HALF), ('rel_keys', (2 * WIN + 1) * DH), ('rel_values', (2 * WIN + 1) * DH)]
    pieces_map = {}
    offset = 0
    for piece_name, piece_width in layout:
        pieces_map[piece_name] = vector[offset:offset + piece_width]
        offset = offset + piece_width
    return pieces_map

def unpack(flats):
    return {'qkv': flats[0].reshape(H, 3 * H), 'out': flats[1].reshape(H, H), 'ffn_in': flats[2].reshape(KFF * H, FF), 'ffn_out': flats[3].reshape(KFF * FF, H), 'pre': flats[4].reshape(HALF, H), 'gate': flats[5].reshape(KWN * H, GATES), 'skip': flats[6].reshape(H, H), 'post': flats[7].reshape(H, HALF), 'vector': vector_parts(flats[8])}

def shifted(values, segments, offset):
    if offset == 0:
        return values
    margin = abs(offset)
    count_rows = values.shape[0]
    padded = jnp.pad(values, ((margin, margin), (0, 0)))
    seg_padded = jnp.pad(segments, (margin, margin), constant_values=-1)
    moved = lax.slice_in_dim(padded, margin + offset, margin + offset + count_rows, axis=0)
    moved_seg = lax.slice_in_dim(seg_padded, margin + offset, margin + offset + count_rows, axis=0)
    return jnp.where((moved_seg == segments)[:, None], moved, jnp.zeros_like(moved))

def columns(values, segments, kernel):
    center = (kernel - 1) // 2
    return jnp.concatenate([shifted(values, segments, tap - center) for tap in range(kernel)], axis=1)

def band_place(values, count_rows):
    heads_count = values.shape[0]
    wide = jnp.pad(values, ((0, 0), (0, 0), (0, count_rows)))
    flat = wide.reshape(heads_count, count_rows * (count_rows + 2 * WIN + 1))
    flat = flat[:, :count_rows * (count_rows + 2 * WIN)]
    return flat.reshape(heads_count, count_rows, count_rows + 2 * WIN)[:, :, WIN:WIN + count_rows]

def band_take(matrix):
    heads_count = matrix.shape[0]
    count_rows = matrix.shape[2]
    padded = jnp.pad(matrix, ((0, 0), (0, 0), (WIN, WIN)))
    flat = padded.reshape(heads_count, count_rows * (count_rows + 2 * WIN))
    flat = jnp.pad(flat, ((0, 0), (0, count_rows)))
    return flat.reshape(heads_count, count_rows, count_rows + 2 * WIN + 1)[:, :, :2 * WIN + 1]

def layer_norm(values, gain, bias):
    centered = values - lax.optimization_barrier(jnp.mean(values, axis=-1, keepdims=True))
    variance = lax.optimization_barrier(jnp.mean(centered * centered, axis=-1, keepdims=True))
    return centered * lax.rsqrt(variance + 1e-05) * gain + bias

def gate_mix(values):
    return jnp.tanh(values[:, :H]) * jax.nn.sigmoid(values[:, H:])

def layer(inputs_row, segments, weights):
    pieces_map = weights['vector']
    count_rows = inputs_row.shape[0]
    bias_qkv = jnp.concatenate([pieces_map['q_bias'], jnp.zeros((H,), jnp.float32), pieces_map['v_bias']])
    qkv = low(low_back(matmul(inputs_row, weights['qkv']) + bias_qkv))
    heads_all = qkv.reshape(count_rows, 3, HEADS, DH).transpose(1, 2, 0, 3)
    queries, keys_all, values_all = (heads_all[0], heads_all[1], heads_all[2])
    rel_keys = pieces_map['rel_keys'].reshape(2 * WIN + 1, DH)
    rel_values = pieces_map['rel_values'].reshape(2 * WIN + 1, DH)
    scale = DH ** (-0.5)
    near_terms = jnp.einsum('hid,rd->hir', queries, rel_keys, precision=highest)
    raw_scores = (jnp.einsum('hid,hjd->hij', queries, keys_all, precision=highest) + band_place(near_terms, count_rows)) * scale
    scores = low_back(raw_scores)
    same_seg = (segments[:, None] == segments[None, :])[None]
    masked = jnp.where(same_seg, scores, -1e+30)
    peak = lax.optimization_barrier(jnp.max(masked, axis=-1, keepdims=True))
    expo = jnp.exp(masked - peak)
    probs = expo / lax.optimization_barrier(jnp.sum(expo, axis=-1, keepdims=True))
    probs_low = low(probs)
    context = jnp.einsum('hij,hjd->hid', probs_low, values_all, precision=highest) + jnp.einsum('hir,rd->hid', band_take(probs_low), rel_values, precision=highest)
    context = low(low_back(context.transpose(1, 0, 2).reshape(count_rows, H)))
    attn = low_back(matmul(context, weights['out']) + pieces_map['out_bias'])
    normed = low(layer_norm(inputs_row + attn, pieces_map['norm1_gain'], pieces_map['norm1_bias']))
    hidden = low_back(matmul(columns(normed, segments, KFF), weights['ffn_in']) + pieces_map['ffn_bias1'])
    activated = low(jax.nn.gelu(hidden, approximate=False))
    ffn = low_back(matmul(columns(activated, segments, KFF), weights['ffn_out']) + pieces_map['ffn_bias2'])
    encoded = low(layer_norm(normed + ffn, pieces_map['norm2_gain'], pieces_map['norm2_bias']))
    first_half = encoded[:, :HALF]
    second_half = encoded[:, HALF:]
    start = low(low_back(matmul(first_half, weights['pre']) + pieces_map['pre_bias']))
    gates = low_back(matmul(columns(start, segments, KWN), weights['gate']) + pieces_map['gate_bias'])
    acts = low(gate_mix(gates))
    skip = low(low_back(matmul(acts, weights['skip']) + pieces_map['skip_bias']))
    shift_mean = low_back(matmul(skip, weights['post']) + pieces_map['post_bias'])
    moved = second_half + shift_mean
    return jnp.flip(jnp.concatenate([first_half, moved], axis=1), axis=1)

def reference(inputs, segment_ids, cotangent, qkv_master, out_master, ffn_in_master, ffn_out_master, pre_master, gate_master, skip_master, post_master, vector_master):
    masters = (qkv_master, out_master, ffn_in_master, ffn_out_master, pre_master, gate_master, skip_master, post_master, vector_master)

    def forward(inputs_all, master_list, probe):
        lowered = [low(master) for master in master_list]
        first_weights = unpack([master[0] for master in lowered])
        second_weights = unpack([master[1] for master in lowered])

        def row_pair(items):
            inputs_row, seg_row, probe_row = items
            hidden_row = low(layer(inputs_row, seg_row, first_weights))
            passed = low_back(hidden_row + probe_row)
            return (hidden_row, layer(passed, seg_row, second_weights))
        return lax.map(jax.checkpoint(row_pair), (inputs_all, segment_ids, probe))
    inputs_all = inputs.astype(jnp.float32)
    probe = jnp.zeros_like(inputs_all)
    (hidden_rows, final_rows), pullback = jax.vjp(forward, inputs_all, list(masters), probe)
    grad_inputs, grad_masters, grad_probe = pullback((jnp.zeros_like(hidden_rows), cotangent))
    layer_outputs = jnp.stack([hidden_rows, final_rows]).astype(jnp.bfloat16)
    input_grads = jnp.stack([grad_inputs, grad_probe])
    return (layer_outputs, input_grads, grad_masters[0], grad_masters[1], grad_masters[2], grad_masters[3], grad_masters[4], grad_masters[5], grad_masters[6], grad_masters[7], grad_masters[8])
```

```python
import jax
import jax.numpy as jnp
from jax import lax
from jax.experimental import pallas as pl
from jax.experimental.pallas import tpu as pltpu
from jax.sharding import PartitionSpec as P

H = 192
HEADS = 2
FF = 768
KFF = 3
KWN = 5
WIN = 4
DH = 96
GATES = 384
HALF = 96
BAND = 2 * WIN + 1
CHUNKS = 16
WIDE = 384
ROWS_A = 32
ROWS_F = 144
ROWS_C = 80
VROWS = 32
ONE = H + 16
SCALE = DH**-0.5
BF = jnp.bfloat16
F32 = jnp.float32
LANE = 128


def nn(a, b):
    return lax.dot_general(a, b, (((1,), (0,)), ((), ())), preferred_element_type=F32)


def nt(a, b):
    return lax.dot_general(a, b, (((1,), (1,)), ((), ())), preferred_element_type=F32)


def tn(a, b):
    return lax.dot_general(a, b, (((0,), (0,)), ((), ())), preferred_element_type=F32)


def call(body, outs, args, scratch=(), limit=48):
    spec = pl.BlockSpec(memory_space=pltpu.VMEM)
    return pl.pallas_call(
        body,
        out_shape=[jax.ShapeDtypeStruct(shape, kind) for shape, kind in outs],
        in_specs=[spec] * len(args),
        out_specs=[spec] * len(outs),
        scratch_shapes=[pltpu.VMEM(shape, kind) for shape, kind in scratch],
        compiler_params=pltpu.CompilerParams(vmem_limit_bytes=limit * 1024 * 1024),
    )(*args)


def rows_to(values, rows):
    return jnp.pad(values, ((0, 0), (0, rows - values.shape[1]), (0, 0)))


def pack(flats):
    qkv, out, ffn_in, ffn_out, pre, gate, skip, post, vec = flats
    n = qkv.shape[0]
    qkv = qkv.reshape(n, -1, 3 * H)
    out = out.reshape(n, -1, H)
    ffn_in = ffn_in.reshape(n, -1, FF)
    ffn_out = ffn_out.reshape(n, -1, H)
    pre = pre.reshape(n, -1, H)
    gate = gate.reshape(n, -1, GATES)
    skip = skip.reshape(n, -1, H)
    post = post.reshape(n, -1, HALF)
    half = ffn_out.shape[1] // 2
    part_a = jnp.concatenate(
        [
            rows_to(qkv[:, :, :WIDE], 16),
            rows_to(jnp.concatenate([qkv[:, :, WIDE:], out], axis=2), 12),
            vec.reshape(n, 1, WIDE),
        ],
        axis=1,
    )
    part_f = jnp.concatenate(
        [
            ffn_in[:, :, :WIDE],
            ffn_in[:, :, WIDE:],
            jnp.concatenate([ffn_out[:, :half], ffn_out[:, half:]], axis=2),
        ],
        axis=1,
    )
    post = jnp.pad(post, ((0, 0), (0, 0), (0, H - HALF)))
    pre = jnp.pad(pre, ((0, 0), (0, 0), (0, H)))
    part_c = jnp.concatenate([gate, jnp.concatenate([skip, post], axis=2), pre], axis=1)
    return (rows_to(part_a, ROWS_A), part_f, rows_to(part_c, ROWS_C))


def unpack(part_a, part_f, part_c):
    n = part_a.shape[0]
    h12, h36, h60 = H // CHUNKS, KFF * H // CHUNKS, KWN * H // CHUNKS
    qkv = jnp.concatenate([part_a[:, :h12], part_a[:, 16 : 16 + h12, :H]], axis=2)
    out = part_a[:, 16 : 16 + h12, H:]
    vec = part_a[:, 28]
    ffn_in = jnp.concatenate([part_f[:, :h36], part_f[:, h36 : 2 * h36]], axis=2)
    low = part_f[:, 2 * h36 :]
    ffn_out = jnp.concatenate([low[:, :, :H], low[:, :, H:]], axis=1)
    gate = part_c[:, :h60]
    skip = part_c[:, h60 : h60 + h12, :H]
    post = part_c[:, h60 : h60 + h12, H : H + HALF]
    pre = part_c[:, h60 + h12 : h60 + h12 + HALF // CHUNKS, :H]
    return tuple(
        x.reshape(n, -1) for x in (qkv, out, ffn_in, ffn_out, pre, gate, skip, post, vec)
    )


def rebuild_a(pa, wqkv, wo, vec, stage):
    stage[...] = jnp.zeros(stage.shape, F32)
    for b in range(CHUNKS):
        x = pa[b].astype(F32)
        r = slice(12 * b, 12 * b + 12)
        stage[r, :WIDE] = x[:12]
        stage[r, WIDE : 2 * WIDE] = x[16:28]
        vec[2 * b : 2 * b + 1, :] = x[28:29, :H]
        vec[2 * b + 1 : 2 * b + 2, :] = x[28:29, H:]
    stage[H : H + 1, :H] = vec[0:1, :]
    stage[H : H + 1, WIDE : WIDE + H] = vec[1:2, :]
    wqkv[...] = stage[:ONE, : 3 * H].astype(BF)
    wo[:H, :] = stage[:H, 3 * H :].astype(BF)
    pad = lax.broadcasted_iota(jnp.int32, (16, H), 0)
    wo[H:, :] = jnp.where(pad == 0, vec[2:3, :], 0.0).astype(BF)


def rebuild_f(pf, vec, w1, w2, stage1, stage2):
    for b in range(CHUNKS):
        x = pf[b].astype(F32)
        r = slice(36 * b, 36 * b + 36)
        stage1[r, :WIDE] = x[:36]
        stage1[r, WIDE:] = x[36:72]
        w2[144 * b : 144 * b + 72, :] = x[72:, :H].astype(BF)
        stage2[...] = x[72:, H:]
        w2[144 * b + 72 : 144 * b + 144, :] = stage2[...].astype(BF)
    w1[: KFF * H, :] = stage1[...].astype(BF)
    pad = lax.broadcasted_iota(jnp.int32, (16, H), 0)
    for k in range(4):
        w1[KFF * H :, H * k : H * k + H] = jnp.where(pad == 0, vec[5 + k : 6 + k, :], 0.0).astype(BF)


def rebuild_c(pc, vec, wg, wskip, wpost, wpre, stage):
    n = KWN * H
    wide = lax.broadcasted_iota(jnp.int32, (16, ONE), 0)
    lane = lax.broadcasted_iota(jnp.int32, (16, ONE), 1)
    corner = ((wide == 0) & (lane == H)).astype(F32)
    pad = lax.broadcasted_iota(jnp.int32, (16, H), 0) == 0
    stage[...] = jnp.zeros(stage.shape, F32)
    for b in range(CHUNKS):
        x = pc[b].astype(F32)
        stage[60 * b : 60 * b + 60, :] = x[:60]
        stage[n + 12 * b : n + 12 * b + 12, :] = x[60:72]
        stage[n + H + 6 * b : n + H + 6 * b + 6, :] = x[72:78]
    wg[:n, :] = stage[:n, :].astype(BF)
    wg[n:, :H] = jnp.where(pad, vec[13:14, :], 0.0).astype(BF)
    wg[n:, H:] = jnp.where(pad, vec[14:15, :], 0.0).astype(BF)
    wskip[...] = jnp.zeros(wskip.shape, BF)
    wpre[...] = jnp.zeros(wpre.shape, BF)
    wskip[H:, :] = corner.astype(BF)
    wpre[H:, :] = corner.astype(BF)
    wskip[:H, :H] = stage[n : n + H, :H].astype(BF)
    wskip[H:, :H] = jnp.where(pad, vec[15:16, :], 0.0).astype(BF)
    wpost[:H, :] = stage[n : n + H, H : H + HALF].astype(BF)
    wpost[H:, :] = jnp.where(pad, vec[16:17, :], 0.0)[:, :HALF].astype(BF)
    wpre[:HALF, :H] = stage[n + H : n + H + HALF, :H].astype(BF)
    wpre[H:, :H] = jnp.where(pad, vec[12:13, :], 0.0).astype(BF)


def column(row):
    return jnp.transpose(jnp.broadcast_to(row, (LANE, row.shape[1])))


def embeddings(vec, first):
    rows = []
    for r in range(BAND):
        at = first + r
        piece = vec[at // 2 : at // 2 + 1, :]
        rows.append(piece[:, :HALF] if at % 2 == 0 else piece[:, HALF:])
    index = lax.broadcasted_iota(jnp.int32, (16, HALF), 0)
    total = jnp.zeros((16, HALF), F32)
    for r in range(BAND):
        total = jnp.where(index == r, rows[r], total)
    return total


def one_rows(frames):
    return (lax.broadcasted_iota(jnp.int32, (16, frames), 0) == 0).astype(BF)


def moved(x, masks, offset):
    if offset == 0:
        return x
    frames = x.shape[1]
    row = {-2: 0, -1: 1, 1: 2, 2: 3}[offset]
    return pltpu.roll(x, (-offset) % frames, 1) * masks[row : row + 1, :]


def skewed(near):
    s = lax.broadcasted_iota(jnp.int32, (8, LANE), 0)
    l = lax.broadcasted_iota(jnp.int32, (8, LANE), 1)
    index = (s - l + WIN) & 7
    total = jnp.zeros((8, LANE), F32)
    for r in range(8):
        total = jnp.where(index == r, near[r : r + 1, :], total)
    return total


def unskewed(kept):
    r = lax.broadcasted_iota(jnp.int32, (8, LANE), 0)
    l = lax.broadcasted_iota(jnp.int32, (8, LANE), 1)
    index = (r + l - WIN) & 7
    total = jnp.zeros((8, LANE), F32)
    for s in range(8):
        total = jnp.where(index == s, kept[s : s + 1, :], total)
    return total


def span(block, frames):
    return max(0, LANE * block - 8), min(frames, LANE * block + LANE + 8)


def reach(block, frames):
    low, high = span(block, frames)
    j = lax.broadcasted_iota(jnp.int32, (high - low, LANE), 0) + (low - LANE * block)
    return j - lax.broadcasted_iota(jnp.int32, (high - low, LANE), 1) + WIN


def band_place(near, block, frames):
    r = reach(block, frames)
    count = r.shape[0]
    tiled = jnp.broadcast_to(skewed(near)[None], (count // 8, 8, LANE)).reshape(count, LANE)
    placed = jnp.where((r >= 0) & (r < 8), tiled, 0.0)
    return jnp.where(r == 8, near[8:9, :], placed)


def band_take(piece, block, frames):
    r = reach(block, frames)
    count = r.shape[0]
    kept = jnp.where((r >= 0) & (r < 8), piece, 0.0).reshape(count // 8, 8, LANE).sum(axis=0)
    last = jnp.sum(jnp.where(r == 8, piece, 0.0), axis=0, keepdims=True)
    first = lax.broadcasted_iota(jnp.int32, (8, LANE), 0) == 0
    return jnp.concatenate([unskewed(kept), jnp.where(first, last, 0.0)], axis=0)


def norm_block(x, gain, bias):
    mean = jnp.sum(x, axis=0, keepdims=True) * (1.0 / H)
    centered = x - mean
    variance = jnp.sum(centered * centered, axis=0, keepdims=True) * (1.0 / H)
    rstd = lax.rsqrt(variance + 1e-05)
    xhat = centered * rstd
    return xhat * gain + bias, xhat, rstd


def norm_back(g, gain, xhat, rstd):
    gx = g * gain
    m1 = jnp.sum(gx, axis=0, keepdims=True) * (1.0 / H)
    m2 = jnp.sum(gx * xhat, axis=0, keepdims=True) * (1.0 / H)
    return rstd * (gx - m1 - xhat * m2)


def lane_sums(x):
    ones = jnp.ones((8, LANE), F32)
    total = lax.dot_general(
        ones, x, (((1,), (1,)), ((), ())), precision=lax.Precision.HIGHEST, preferred_element_type=F32
    )
    return total[:1]


def attn_fwd(u, seg, segcol, masks, pa, qkv, probs, ctx, xhat, rstd, ncols, wqkv, wo, vec, stage, score, scratch):
    frames = u.shape[1]
    rebuild_a(pa, wqkv, wo, vec, stage)
    x = jnp.concatenate([u[...], one_rows(frames)], axis=0)
    qkv[...] = tn(wqkv[...], x).astype(BF)
    ek = embeddings(vec, 33).astype(BF)
    ev = embeddings(vec, 42).astype(BF)
    for h in range(HEADS):
        q = qkv[DH * h : DH * h + DH, :]
        k = qkv[H + DH * h : H + DH * h + DH, :]
        v = qkv[2 * H + DH * h : 2 * H + DH * h + DH, :]
        score[...] = tn(k, q)
        near = nn(ek, q)
        bands = []
        for block in range(frames // LANE):
            cols = slice(LANE * block, LANE * block + LANE)
            low, high = span(block, frames)
            score[low:high, cols] += band_place(near[:, cols], block, frames)
            same = segcol[...] == seg[:, cols]
            s = jnp.where(same, score[:, cols] * SCALE, -1e30)
            e = jnp.exp(s - jnp.max(s, axis=0, keepdims=True))
            p = (e * (1.0 / jnp.sum(e, axis=0, keepdims=True))).astype(BF)
            probs[h, :, cols] = p
            bands.append(band_take(p[low:high, :].astype(F32), block, frames))
        band = jnp.concatenate(bands, axis=1).astype(BF)
        ctx[DH * h : DH * h + DH, :] = (nn(v, probs[h]) + tn(ev, band)).astype(BF)
    ctx[H:, :] = one_rows(frames)
    scratch[...] = u[...].astype(F32) + tn(wo[...], ctx[...])
    gain, bias = column(vec[3:4, :]), column(vec[4:5, :])
    for block in range(frames // LANE):
        cols = slice(LANE * block, LANE * block + LANE)
        y, xh, rs = norm_block(scratch[:, cols], gain, bias)
        xhat[:, cols] = xh
        rstd[:, cols] = jnp.broadcast_to(rs, (8, LANE))
        scratch[:, cols] = y.astype(BF).astype(F32)
    y = scratch[...]
    ncols[:H, :] = moved(y, masks, -1).astype(BF)
    ncols[H : 2 * H, :] = y.astype(BF)
    ncols[2 * H : 3 * H, :] = moved(y, masks, 1).astype(BF)
    ncols[3 * H :, :] = one_rows(frames)


def ffn_fwd(ncols, masks, pf, vec, act, dact, xhat, rstd, enc, w1, w2, stage1, stage2, wide, scratch):
    frames = ncols.shape[1]
    rebuild_f(pf, vec, w1, w2, stage1, stage2)
    wide[...] = tn(w1[...], ncols[...])

    def gelu_rows(step, carry):
        rows = pl.ds(pl.multiple_of(step * 32, 32), 32)
        x = wide[rows, :]
        phi = 0.5 + 0.5 * lax.erf(x * 0.7071067811865476)
        density = jnp.exp(-0.5 * x * x) * 0.3989422804014327
        act[rows, :] = (x * phi).astype(BF)
        dact[rows, :] = (phi + x * density).astype(BF)
        return carry

    lax.fori_loop(0, FF // 32, gelu_rows, 0)
    total = ncols[H : 2 * H, :].astype(F32)
    for tap in range(KFF):
        y = tn(w2[FF * tap : FF * tap + FF, :], act[...])
        total = total + moved(y, masks, tap - 1)
    scratch[...] = total
    gain, bias, extra = column(vec[10:11, :]), column(vec[11:12, :]), column(vec[9:10, :])
    for block in range(frames // LANE):
        cols = slice(LANE * block, LANE * block + LANE)
        y, xh, rs = norm_block(scratch[:, cols] + extra, gain, bias)
        xhat[:, cols] = xh
        rstd[:, cols] = jnp.broadcast_to(rs, (8, LANE))
        enc[:H, cols] = y.astype(BF)
    enc[H:, :] = one_rows(frames)


def flip_matrix():
    r = lax.broadcasted_iota(jnp.int32, (H, H), 0)
    c = lax.broadcasted_iota(jnp.int32, (H, H), 1)
    return (r + c == H - 1).astype(BF)


def coup_fwd(enc, masks, pc, vec, scols, acts, da, db, skip, out, wg, wskip, wpost, wpre, stage):
    frames = enc.shape[1]
    n = KWN * H
    rebuild_c(pc, vec, wg, wskip, wpost, wpre, stage)
    start = tn(wpre[...], enc[...]).astype(BF).astype(F32)[:H]
    for tap in range(KWN):
        scols[H * tap : H * tap + H, :] = moved(start, masks, tap - 2).astype(BF)
    scols[n:, :] = one_rows(frames)
    gates = tn(wg[...], scols[...])
    t = jnp.tanh(gates[:H])
    s = 0.5 + 0.5 * jnp.tanh(0.5 * gates[H:])
    acts[:H, :] = (t * s).astype(BF)
    acts[H:, :] = one_rows(frames)
    da[...] = ((1.0 - t * t) * s).astype(BF)
    db[...] = (t * s * (1.0 - s)).astype(BF)
    skip[...] = tn(wskip[...], acts[...]).astype(BF)
    shift = tn(wpost[...], skip[...])
    low = (enc[HALF:H, :].astype(F32) + shift).astype(BF)
    cat = jnp.concatenate([enc[:HALF, :], low], axis=0)
    out[...] = nn(flip_matrix(), cat).astype(BF)


def coup_bwd(gout, enc, scols, acts, da, db, skip, masks, wg, wskip, wpost, wpre, genc, gc, gvec, stage, piece, tall):
    n = KWN * H
    flip = flip_matrix()
    g = gout[...]
    if g.dtype == F32:
        high = g.astype(BF)
        gcat = nn(flip, high) + nn(flip, (g - high.astype(F32)).astype(BF))
    else:
        gcat = nn(flip, g)
    gmean = gcat[HALF:].astype(BF)
    gpost = nt(skip[...], gmean)
    gskip = nn(wpost[:H, :], gmean).astype(BF)
    gsk = nt(acts[...], gskip)
    gacts = nn(wskip[:H, :H], gskip)
    ggates = jnp.concatenate(
        [(gacts * da[...].astype(F32)).astype(BF), (gacts * db[...].astype(F32)).astype(BF)], axis=0
    )
    stage[: n + 16, :] = nt(scols[...], ggates)
    tall[...] = nn(wg[:n, :], ggates)
    total = tall[2 * H : 3 * H, :]
    for tap in (0, 1, 3, 4):
        total = total + moved(tall[H * tap : H * tap + H, :], masks, 2 - tap)
    gstart = total.astype(BF)
    gpre = nt(enc[...], gstart)
    genc[:HALF, :] = gcat[:HALF] + nn(wpre[:HALF, :H], gstart)
    genc[HALF:, :] = gcat[HALF:]
    gvec[...] = jnp.zeros(gvec.shape, F32)
    gvec[0:1, :] = gpre[H : H + 1, :]
    gvec[1:2, :] = stage[n : n + 1, :H]
    gvec[2:3, :] = stage[n : n + 1, H:]
    gvec[3:4, :] = gsk[H : H + 1, :]
    gvec[4:5, :HALF] = gpost[H : H + 1, :]
    base = n + 16
    stage[base : base + H, :H] = gsk[:H]
    stage[base : base + H, H : H + HALF] = gpost[:H]
    stage[base : base + H, H + HALF :] = jnp.zeros((H, HALF), F32)
    stage[base + H : base + H + HALF, :H] = gpre[:HALF]
    stage[base + H : base + H + HALF, H:] = jnp.zeros((HALF, H), F32)
    piece[...] = jnp.zeros(piece.shape, F32)
    for b in range(CHUNKS):
        piece[:60, :] = stage[60 * b : 60 * b + 60, :]
        piece[60:72, :] = stage[base + 12 * b : base + 12 * b + 12, :]
        piece[72:78, :] = stage[base + H + 6 * b : base + H + 6 * b + 6, :]
        gc[b] = piece[...].astype(gc.dtype)


def ffn_bwd(genc, xhat, rstd, act, dact, ncols, masks, w1, w2, vec, gnorm, gf, gvec, stage1, stage2, piece, wide, gsec):
    frames = genc.shape[1]
    gain = column(vec[10:11, :])
    sums = [jnp.zeros((H, LANE), F32) for _ in range(3)]
    for block in range(frames // LANE):
        cols = slice(LANE * block, LANE * block + LANE)
        g, xh = genc[:, cols], xhat[:, cols]
        d = norm_back(g, gain, xh, rstd[:1, cols])
        gsec[:, cols] = d
        sums[0] = sums[0] + g * xh
        sums[1] = sums[1] + g
        sums[2] = sums[2] + d.astype(BF).astype(F32)
    gvec[...] = jnp.zeros(gvec.shape, F32)
    for row in range(3):
        gvec[row : row + 1, :] = lane_sums(sums[row])
    gffn = gsec[...].astype(BF).astype(F32)
    for tap in range(KFF):
        back = moved(gffn, masks, 1 - tap).astype(BF)
        stage2[FF * tap : FF * tap + FF, :] = nt(act[...], back)
        term = nn(w2[FF * tap : FF * tap + FF, :], back)
        if tap == 0:
            wide[...] = term
        else:
            wide[...] += term
    ghid = (wide[...] * dact[...].astype(F32)).astype(BF)
    stage1[...] = nt(ncols[...], ghid)
    total = gsec[...]
    for tap in range(KFF):
        total = total + moved(nn(w1[H * tap : H * tap + H, :], ghid), masks, 1 - tap)
    gnorm[...] = total
    for k in range(4):
        gvec[3 + k : 4 + k, :] = stage1[KFF * H : KFF * H + 1, H * k : H * k + H]
    for b in range(CHUNKS):
        piece[:36, :] = stage1[36 * b : 36 * b + 36, :WIDE]
        piece[36:72, :] = stage1[36 * b : 36 * b + 36, WIDE:]
        piece[72:, :H] = stage2[144 * b : 144 * b + 72, :]
        piece[72:, H:] = stage2[144 * b + 72 : 144 * b + 144, :]
        gf[b] = piece[...].astype(gf.dtype)


def attn_bwd(
    gnorm, u, qkv, probs, ctx, xhat, rstd, wqkv, wo, vec, gvc, gvf, gin, ga,
    stage, piece, gvec, gfirst, gqkv, dprob,
):
    frames = gnorm.shape[1]
    gain = column(vec[3:4, :])
    sums = [jnp.zeros((H, LANE), F32) for _ in range(2)]
    for block in range(frames // LANE):
        cols = slice(LANE * block, LANE * block + LANE)
        g, xh = gnorm[:, cols], xhat[:, cols]
        gfirst[:, cols] = norm_back(g, gain, xh, rstd[:1, cols])
        sums[0] = sums[0] + g * xh
        sums[1] = sums[1] + g
    gattn = gfirst[...].astype(BF)
    gout = nt(ctx[...], gattn)
    gctx = nn(wo[:H, :], gattn).astype(BF)
    ek = embeddings(vec, 33).astype(BF)
    ev = embeddings(vec, 42).astype(BF)
    gek = jnp.zeros((16, DH), F32)
    gev = jnp.zeros((16, DH), F32)
    for h in range(HEADS):
        q = qkv[DH * h : DH * h + DH, :]
        k = qkv[H + DH * h : H + DH * h + DH, :]
        v = qkv[2 * H + DH * h : 2 * H + DH * h + DH, :]
        gh = gctx[DH * h : DH * h + DH]
        dprob[...] = tn(v, gh)
        near = nn(ev, gh)
        pbands, sbands, ds = [], [], []
        for block in range(frames // LANE):
            cols = slice(LANE * block, LANE * block + LANE)
            low, high = span(block, frames)
            dprob[low:high, cols] += band_place(near[:, cols], block, frames)
            p = probs[h, :, cols].astype(F32)
            d = dprob[:, cols]
            inner = jnp.sum(p * d, axis=0, keepdims=True)
            s = (p * (d - inner)).astype(BF)
            ds.append(s)
            sbands.append(band_take(s[low:high, :].astype(F32), block, frames))
            pbands.append(band_take(p[low:high, :], block, frames))
        ds = jnp.concatenate(ds, axis=1)
        sband = jnp.concatenate(sbands, axis=1).astype(BF)
        pband = jnp.concatenate(pbands, axis=1).astype(BF)
        gek = gek + nt(sband, q)
        gev = gev + nt(pband, gh)
        gqkv[DH * h : DH * h + DH, :] = ((nn(k, ds) + tn(ek, sband)) * SCALE).astype(BF)
        gqkv[H + DH * h : H + DH * h + DH, :] = (nt(q, ds) * SCALE).astype(BF)
        gqkv[2 * H + DH * h : 2 * H + DH * h + DH, :] = nt(gh, probs[h]).astype(BF)
    x = jnp.concatenate([u[...], one_rows(frames)], axis=0)
    stage[...] = nt(x, gqkv[...])
    gin[...] = gfirst[...] + nn(wqkv[:H, :], gqkv[...])
    gvec[...] = jnp.zeros(gvec.shape, F32)
    gvec[0:1, :] = stage[H : H + 1, :H]
    gvec[1:2, :] = stage[H : H + 1, WIDE:]
    gvec[2:3, :] = gout[H : H + 1, :]
    gvec[3:4, :] = lane_sums(sums[0])
    gvec[4:5, :] = lane_sums(sums[1])
    for k in range(4):
        gvec[5 + k : 6 + k, :] = gvf[3 + k : 4 + k, :]
    gvec[9:10, :] = gvf[2:3, :]
    gvec[10:11, :] = gvf[0:1, :]
    gvec[11:12, :] = gvf[1:2, :]
    for k in range(5):
        gvec[12 + k : 13 + k, :] = gvc[k : k + 1, :]
    gek = gek * SCALE
    for r in range(BAND):
        for first, grad in ((33, gek), (42, gev)):
            at = first + r
            if at % 2 == 0:
                gvec[at // 2 : at // 2 + 1, :HALF] = grad[r : r + 1, :]
            else:
                gvec[at // 2 : at // 2 + 1, HALF:] = grad[r : r + 1, :]
    piece[...] = jnp.zeros(piece.shape, F32)
    for b in range(CHUNKS):
        r = slice(12 * b, 12 * b + 12)
        piece[:12, :] = stage[r, :WIDE]
        piece[16:28, :H] = stage[r, WIDE:]
        piece[16:28, H:] = gout[r, :]
        piece[28:29, :H] = gvec[2 * b : 2 * b + 1, :]
        piece[28:29, H:] = gvec[2 * b + 1 : 2 * b + 2, :]
        ga[b] = piece[...].astype(ga.dtype)


def forward(u, seg, segcol, masks, parts):
    frames = u.shape[1]
    pa, pf, pc = parts
    qkv, probs, ctx, xhat1, rstd1, ncols, wqkv, wo, vec = call(
        attn_fwd,
        [
            ((3 * H, frames), BF),
            ((HEADS, frames, frames), BF),
            ((ONE, frames), BF),
            ((H, frames), F32),
            ((8, frames), F32),
            ((KFF * H + 16, frames), BF),
            ((ONE, 3 * H), BF),
            ((ONE, H), BF),
            ((VROWS, H), F32),
        ],
        (u, seg, segcol, masks, pa),
        [((ONE, 2 * WIDE), F32), ((frames, frames), F32), ((H, frames), F32)],
    )
    act, dact, xhat2, rstd2, enc, w1, w2 = call(
        ffn_fwd,
        [
            ((FF, frames), BF),
            ((FF, frames), BF),
            ((H, frames), F32),
            ((8, frames), F32),
            ((ONE, frames), BF),
            ((KFF * H + 16, FF), BF),
            ((KFF * FF, H), BF),
        ],
        (ncols, masks, pf, vec),
        [((KFF * H, FF), F32), ((72, H), F32), ((FF, frames), F32), ((H, frames), F32)],
    )
    scols, acts, da, db, skip, out, wg, wskip, wpost, wpre = call(
        coup_fwd,
        [
            ((KWN * H + 16, frames), BF),
            ((ONE, frames), BF),
            ((H, frames), BF),
            ((H, frames), BF),
            ((ONE, frames), BF),
            ((H, frames), BF),
            ((KWN * H + 16, GATES), BF),
            ((ONE, ONE), BF),
            ((ONE, HALF), BF),
            ((ONE, ONE), BF),
        ],
        (enc, masks, pc, vec),
        [((KWN * H + H + HALF, WIDE), F32)],
    )
    kept = (u, qkv, probs, ctx, xhat1, rstd1, ncols, wqkv, wo, vec, act, dact, xhat2, rstd2, enc, w1, w2)
    return out, kept + (scols, acts, da, db, skip, wg, wskip, wpost, wpre)


def backward(gout, masks, kept, kind):
    (u, qkv, probs, ctx, xhat1, rstd1, ncols, wqkv, wo, vec, act, dact, xhat2, rstd2, enc, w1, w2) = kept[:17]
    scols, acts, da, db, skip, wg, wskip, wpost, wpre = kept[17:]
    frames = gout.shape[1]
    genc, gc, gvc = call(
        coup_bwd,
        [((H, frames), F32), ((CHUNKS, ROWS_C, WIDE), kind), ((8, H), F32)],
        (gout, enc, scols, acts, da, db, skip, masks, wg, wskip, wpost, wpre),
        [((KWN * H + 16 + H + HALF, WIDE), F32), ((ROWS_C, WIDE), F32), ((KWN * H, frames), F32)],
    )
    gnorm, gf, gvf = call(
        ffn_bwd,
        [((H, frames), F32), ((CHUNKS, ROWS_F, WIDE), kind), ((8, H), F32)],
        (genc, xhat2, rstd2, act, dact, ncols, masks, w1, w2, vec),
        [
            ((KFF * H + 16, FF), F32),
            ((KFF * FF, H), F32),
            ((ROWS_F, WIDE), F32),
            ((FF, frames), F32),
            ((H, frames), F32),
        ],
    )
    gin, ga = call(
        attn_bwd,
        [((H, frames), F32), ((CHUNKS, ROWS_A, WIDE), kind)],
        (gnorm, u, qkv, probs, ctx, xhat1, rstd1, wqkv, wo, vec, gvc, gvf),
        [
            ((ONE, 3 * H), F32),
            ((ROWS_A, WIDE), F32),
            ((VROWS, H), F32),
            ((H, frames), F32),
            ((3 * H, frames), BF),
            ((frames, frames), F32),
        ],
    )
    return gin, (ga, gf, gc)


def swap(x):
    return lax.ppermute(x, "section", [(0, 1), (1, 0)])


def on_device(inputs, segment_ids, cotangent, *masters):
    section = lax.axis_index("section")
    first = section == 0
    devices = lax.axis_size("batch")
    length = masters[8].shape[1] * devices
    frames = inputs.shape[1]

    low = [master.astype(BF) for master in masters]
    if devices == CHUNKS:
        own = pack(low)
        both = []
        for part in own:
            other = swap(part)
            both.append((jnp.where(first, part, other), jnp.where(first, other, part)))
        layers = []
        for index in range(2):
            layers.append(
                tuple(lax.all_gather(pair[index], "batch", axis=0, tiled=True) for pair in both)
            )
    else:
        flats = [lax.all_gather(flat, "batch", axis=1, tiled=True) for flat in low]
        flats[8] = flats[8][:, : CHUNKS * WIDE]
        own = pack([flat.reshape(CHUNKS, -1) for flat in flats])
        others = [swap(part) for part in own]
        layers = [
            tuple(jnp.where(first, a, b) for a, b in zip(own, others)),
            tuple(jnp.where(first, b, a) for a, b in zip(own, others)),
        ]

    seg = lax.dynamic_index_in_dim(segment_ids, section, 0, keepdims=True).astype(F32)
    index = jnp.arange(frames)
    rows = []
    for offset in (-2, -1, 1, 2):
        inside = (index + offset >= 0) & (index + offset < frames)
        rows.append(((jnp.roll(seg[0], -offset) == seg[0]) & inside).astype(F32))
    masks = jnp.stack(rows + [jnp.zeros((frames,), F32)] * 4)
    segcol = jnp.broadcast_to(seg[0][:, None], (frames, LANE))

    u0 = lax.dynamic_index_in_dim(inputs, section, 0, keepdims=False).T
    cot = lax.dynamic_index_in_dim(cotangent, section, 0, keepdims=False).T
    out0, kept0 = forward(u0, seg, segcol, masks, layers[0])
    out1, kept1 = forward(out0, seg, segcol, masks, layers[1])
    gin1, parts1 = backward(cot, masks, kept1, BF)
    glow = gin1.astype(BF)
    gin0, parts0 = backward(glow, masks, kept0, BF)

    def section_rows(a0, a1):
        mine = jnp.where(first, a0, a1)
        theirs = swap(jnp.where(first, a1, a0))
        pair = jnp.where(first, jnp.stack([mine, theirs]), jnp.stack([theirs, mine]))
        return pair.transpose(0, 2, 1)[None]

    layer_outputs = section_rows(out0, out1)
    input_grads = section_rows(gin0, glow.astype(F32))

    def total_of(p0, p1):
        if devices != CHUNKS:
            return jnp.where(first, p0, p1).astype(F32) + swap(jnp.where(first, p1, p0)).astype(F32)
        s0 = lax.psum_scatter(p0, "batch", scatter_dimension=0, tiled=True)
        s1 = lax.psum_scatter(p1, "batch", scatter_dimension=0, tiled=True)
        return jnp.where(first, s0, s1).astype(F32) + swap(jnp.where(first, s1, s0)).astype(F32)

    totals = unpack(*(total_of(a, b) for a, b in zip(parts0, parts1)))
    if devices != CHUNKS:
        flats = [flat.reshape(1, -1) for flat in totals]
        flats[8] = jnp.pad(flats[8], ((0, 0), (0, length - flats[8].shape[1])))
        totals = [lax.psum_scatter(flat, "batch", scatter_dimension=1, tiled=True) for flat in flats]
    return (layer_outputs, input_grads, *totals)


def solution(mesh):
    flat = P("section", "batch")
    in_specs = (P("batch", None, None), P("batch", None), P("batch", None, None)) + (flat,) * 9
    rows = P("section", "batch", None, None)
    out_specs = (rows, rows) + (flat,) * 9
    return jax.shard_map(on_device, mesh=mesh, in_specs=in_specs, out_specs=out_specs, check_vma=False)
```
